32 devices in a mesh: dp: 2 (over x), expert: 16 (over z, y, core).
Axes of the slice: x: 2, y: 2, z: 4, core: 2. Of those that a mesh axis runs over, the one named last changes fastest.
Arguments:
- tokens: bfloat16 [256, 2048], P('expert', 'dp'), may hold values from -6 to 6
- cotangent: bfloat16 [256, 2048], P('expert', 'dp'), may hold values from -6 to 6
- expert_ids: int32 [256, 8], P('expert'), may hold values from 0 to 15, all different within a row; in each aligned block of 16 rows (0 to 15, 16 to 31, ...) at most 16 rows name the same one
- gate_probs: float32 [256, 8], P('expert'), may hold values from 0.05 to 1
- w_gate: bfloat16 [16, 768, 2048], P('expert', None, 'dp'), may hold values from -0.125 to 0.125
- w_up: bfloat16 [16, 768, 2048], P('expert', None, 'dp'), may hold values from -0.125 to 0.125
- w_down: bfloat16 [16, 768, 2048], P('expert', None, 'dp'), may hold values from -0.21875 to 0.21875
Outputs:
- mixed: bfloat16 [256, 2048], P('expert', 'dp')
- grad_tokens: bfloat16 [256, 2048], P('expert', 'dp')
- grad_gate: bfloat16 [16, 768, 2048], P('expert', None, 'dp')
- grad_up: bfloat16 [16, 768, 2048], P('expert', None, 'dp')
- grad_down: bfloat16 [16, 768, 2048], P('expert', None, 'dp')
The draws below stay inside these ranges and needn't reach their ends.
Inputs may be any that keep to these rules, and one draw needn't show every extreme that they name: `expert_ids`: each token names 8 different experts. The 16 tokens of one index of expert (rows b * 16 to (b + 1) * 16 - 1) name no expert more than 16 times, a bound that some block reaches.
All inputs are finite; a program needn't handle non-finite values.
Results may differ from the reference program's by a relative error of at most 0.02.
Values may be sent and summed in bfloat16 or wider, within the bound.
No kernel may reach another device: no remote copies, remote signals or barrier semaphores. Data moves between devices by JAX's collectives and lax.ppermute only.
A program may use at most 64 MiB of HBM per device.

```python
import math
import jax
import jax.numpy as jnp
import numpy as np
from jax import lax

D = 2048
FF = 768
TOPK = 8
TOK_DEV = 16
EXPERTS = 16
CAP = 16
TOKENS = 256
N_DP = 2


def block_scale(own_key, extent, shards, low, top_value):
    def one(axis_at, blocks):
        draws = jax.random.uniform(jax.random.fold_in(jax.random.fold_in(own_key, 6), axis_at), (blocks,), jnp.float32, low / len(shards), top_value / len(shards))
        return jnp.repeat(jnp.exp(draws), extent[axis_at] // blocks).reshape((-1,) + (1,) * (len(extent) - axis_at - 1))

    level = one(*shards[0])
    for cut in shards[1:]:
        level = level * one(*cut)
    return level


def routed_block(rng, own, number, rows, number_of, top, most, slope):
    order = jax.random.permutation(rng, number_of)
    crowded, common = shares(number_of, rows * top, most, slope, True), shares(number_of, rows * top, most, slope, False)
    places = jnp.arange(number_of)

    def named(lengths, rotation):
        used = int((lengths > 0).sum())
        fixed = max(1, used // 4)
        passed = fixed + (places - fixed + rotation * (used - fixed)) % max(1, number_of - fixed)
        return jnp.zeros((number_of,), jnp.int32).at[order[jnp.where(places < fixed, places, passed)]].set(jnp.asarray(lengths, jnp.int32))

    lengths = jnp.where(number % 4 == 0, named(crowded, number // 4), named(common, number - number // 4 - 1))
    mixed = jax.random.permutation(jax.random.fold_in(own, 3), number_of)
    giver, receiver = mixed[0:number_of // 2 * 2:2], mixed[1:number_of // 2 * 2:2]
    margin = jnp.minimum(lengths[giver] - 1, most - lengths[receiver]) // 2
    margin = jnp.where((giver == order[0]) | (receiver == order[0]) | (lengths[receiver] == 0), 0, jnp.maximum(margin, 0))
    passed = jax.random.randint(jax.random.fold_in(own, 4), (number_of // 2,), 0, 1 << 20) % (margin + 1)
    lengths = lengths.at[giver].add(-passed).at[receiver].add(passed)
    members = jnp.searchsorted(jnp.cumsum(lengths), jnp.arange(rows * top), side="right").astype(jnp.int32)
    listing = members.reshape(top, rows).T
    listing = listing[jax.random.permutation(jax.random.fold_in(own, 1), rows)]
    rotation = jax.random.randint(jax.random.fold_in(own, 2), (rows, 1), 0, top)
    return jnp.take_along_axis(listing, (jnp.arange(top)[None, :] + rotation) % top, axis=1)


def shares(count, total, most, lean, full):
    portions = [(1 << 20) // math.isqrt(rank ** lean) + 1 for rank in range(1, count + 1)]
    largest = most if full else min(most, max(-(-total // count), total * portions[0] // sum(portions)))
    least = 1 if total - largest >= count - 1 else 0
    counts, rest = [largest] + [least] * (count - 1), total - largest - least * (count - 1)
    while rest > 0:
        movable = [i for i in range(1, count) if counts[i] < largest] or [i for i in range(1, count) if counts[i] < most]
        mass, left = sum([portions[i] for i in movable]), rest
        for i in movable:
            addition = min(most - counts[i], max(1, left * portions[i] // mass), rest)
            counts[i] = counts[i] + addition
            rest = rest - addition
    return np.array(counts)


def centred(key, dims, scale, most, pieces=(), kind=jnp.bfloat16):
    values = scale * jax.random.normal(key, dims, jnp.float32)
    if pieces:
        values = values * block_scale(key, dims, pieces, -0.22, 0.18)
    return jnp.clip(values, -most, most).astype(kind)


def setup_inputs(seed: int = 0) -> dict:
    splits = jax.random.split(jax.random.key(seed), 8)
    tokens = centred(splits[0], (TOKENS, D), 1.0, 6.0, ((0, 16), (1, 2)))
    cotangent = centred(splits[1], (TOKENS, D), 1.0, 6.0, ((0, 16), (1, 2)))
    expert_ids_keys = jax.random.split(jax.random.fold_in(splits[2], 1), TOKENS // TOK_DEV)
    expert_ids_turns = jax.random.permutation(jax.random.fold_in(splits[2], 3), TOKENS // TOK_DEV)
    expert_ids = jax.vmap(lambda own, number: routed_block(jax.random.fold_in(splits[2], 2), own, number, TOK_DEV, EXPERTS, TOPK, CAP, 2))(expert_ids_keys, expert_ids_turns).reshape((TOKENS, TOPK))
    gate_probs = jnp.clip(jnp.exp(math.log(1.0) - 2.9957323 * jax.random.uniform(splits[3], (TOKENS, TOPK), jnp.float32) ** block_scale(splits[3], (TOKENS, TOPK), ((0, 16),), -0.2, 0.2)), 0.05, 1.0)
    w_gate = centred(splits[4], (EXPERTS, FF, D), D ** -0.5, 0.125, ((0, 16), (2, 2)))
    w_up = centred(splits[5], (EXPERTS, FF, D), D ** -0.5, 0.125, ((0, 16), (2, 2)))
    w_down = centred(splits[6], (EXPERTS, FF, D), FF ** -0.5, 0.21875, ((0, 16), (2, 2)))
    return {"tokens": tokens, "cotangent": cotangent, "expert_ids": expert_ids, "gate_probs": gate_probs, "w_gate": w_gate, "w_up": w_up, "w_down": w_down}


def activate(pre_gate, pre_up, back_hidden):
    sigmas = jax.nn.sigmoid(pre_gate)
    silu_vals = pre_gate * sigmas
    hidden = (silu_vals * pre_up).astype(jnp.bfloat16)
    back_gate = (back_hidden * pre_up * sigmas * (1.0 + pre_gate * (1.0 - sigmas))).astype(jnp.bfloat16)
    back_up = (back_hidden * silu_vals).astype(jnp.bfloat16)
    return hidden, back_gate, back_up


def block_sums(rows, matrix):
    count = rows.shape[0]
    width = D // N_DP
    left = rows.astype(jnp.float32).reshape(count, N_DP, width)
    right = matrix.astype(jnp.float32).reshape(matrix.shape[0], N_DP, width)
    parts = jnp.einsum("snd,fnd->nsf", left, right, precision=lax.Precision.HIGHEST)
    parts = parts.astype(jnp.bfloat16).astype(jnp.float32)
    return jnp.sum(parts, axis=0)


def reference(tokens, cotangent, expert_ids, gate_probs, w_gate, w_up, w_down):
    blocks = TOKENS // TOK_DEV
    chosen = expert_ids.reshape(blocks, TOK_DEV * TOPK).astype(jnp.int32)
    onehot = (chosen[:, :, None] == jnp.arange(EXPERTS, dtype=jnp.int32)[None, None, :]).astype(jnp.int32)
    before = jnp.cumsum(onehot, axis=1) - onehot
    ranks = jnp.sum(before * onehot, axis=2).astype(jnp.int32)
    block_ids = jnp.broadcast_to(jnp.arange(blocks, dtype=jnp.int32)[:, None], chosen.shape)
    token_ids = block_ids * TOK_DEV + (jnp.arange(TOK_DEV * TOPK, dtype=jnp.int32) // TOPK)[None, :]
    slot_table = jnp.full((EXPERTS, blocks, CAP), TOKENS, jnp.int32).at[chosen, block_ids, ranks].set(token_ids)
    prob_table = jnp.zeros((EXPERTS, blocks, CAP), jnp.float32).at[chosen, block_ids, ranks].set(
        gate_probs.reshape(blocks, TOK_DEV * TOPK).astype(jnp.float32))
    padded_x = jnp.concatenate([tokens, jnp.zeros((1, D), tokens.dtype)], axis=0)
    padded_dy = jnp.concatenate([cotangent.astype(jnp.float32), jnp.zeros((1, D), jnp.float32)], axis=0)
    contract_rows = (((0,), (0,)), ((), ()))

    def one_expert(packed):
        row_ids, row_probs, gate_mat, up_mat, down_mat = packed
        row_ids = row_ids.reshape(-1)
        row_probs = row_probs.reshape(-1)
        x_rows = padded_x[row_ids]
        back_row = (row_probs[:, None] * padded_dy[row_ids]).astype(jnp.bfloat16)
        pre_gate = block_sums(x_rows, gate_mat)
        pre_up = block_sums(x_rows, up_mat)
        back_hidden = block_sums(back_row, down_mat)
        hidden, back_gate, back_up = activate(pre_gate, pre_up, back_hidden)
        expert_out = jnp.dot(hidden, down_mat, preferred_element_type=jnp.float32).astype(jnp.bfloat16)
        back_rows = (jnp.dot(back_gate, gate_mat, preferred_element_type=jnp.float32)
                     + jnp.dot(back_up, up_mat, preferred_element_type=jnp.float32)).astype(jnp.bfloat16)
        grad_gate = lax.dot_general(back_gate, x_rows, contract_rows, preferred_element_type=jnp.float32).astype(jnp.bfloat16)
        grad_up = lax.dot_general(back_up, x_rows, contract_rows, preferred_element_type=jnp.float32).astype(jnp.bfloat16)
        grad_down = lax.dot_general(hidden, back_row, contract_rows, preferred_element_type=jnp.float32).astype(jnp.bfloat16)
        return expert_out, back_rows, grad_gate, grad_up, grad_down

    expert_out, back_rows, grad_gate, grad_up, grad_down = lax.map(
        one_expert, (slot_table, prob_table, w_gate, w_up, w_down))
    flat_rows = slot_table.reshape(-1)
    flat_probs = prob_table.reshape(-1)
    mixed = jnp.zeros((TOKENS + 1, D), jnp.float32).at[flat_rows].add(
        flat_probs[:, None] * expert_out.reshape(-1, D).astype(jnp.float32))
    grad_tokens = jnp.zeros((TOKENS + 1, D), jnp.float32).at[flat_rows].add(
        back_rows.reshape(-1, D).astype(jnp.float32))
    return (mixed[:TOKENS].astype(jnp.bfloat16), grad_tokens[:TOKENS].astype(jnp.bfloat16),
            grad_gate, grad_up, grad_down)
```

```python
import functools

import jax
import jax.numpy as jnp
from jax import lax
from jax.experimental import pallas as pl
from jax.experimental.pallas import tpu as pltpu
from jax.sharding import PartitionSpec as P

VMEM = pl.BlockSpec(memory_space=pltpu.VMEM)
NT = (((1,), (1,)), ((), ()))
NN = (((1,), (0,)), ((), ()))
TN = (((0,), (0,)), ((), ()))


def dot(a, b, dims):
    return lax.dot_general(a, b, dims, preferred_element_type=jnp.float32)


def partial_kernel(rows_ref, gate_ref, up_ref, down_ref, out_ref):
    ff, cols = gate_ref.shape
    x = rows_ref[:, :cols]
    d = rows_ref[:, cols : 2 * cols]
    out_ref[:, :ff] = dot(x, gate_ref[...], NT).astype(out_ref.dtype)
    out_ref[:, ff : 2 * ff] = dot(x, up_ref[...], NT).astype(out_ref.dtype)
    out_ref[:, 2 * ff :] = dot(d, down_ref[...], NT).astype(out_ref.dtype)


def post_kernel(experts, own_ref, other_ref, rows_ref, pick_ref, gate_ref, up_ref, down_ref, out_ref, act_ref):
    ff, cols = gate_ref.shape
    prob = jnp.sum(
        rows_ref[:, 2 * cols :].astype(jnp.float32) * pick_ref[...], axis=1, keepdims=True
    )
    both = own_ref[...].astype(jnp.float32) + other_ref[...].astype(jnp.float32)
    pre_gate = both[:, :ff]
    pre_up = both[:, ff : 2 * ff]
    back_hidden = both[:, 2 * ff :] * prob
    s = 1.0 / (1.0 + jnp.exp(-pre_gate))
    silu = pre_gate * s
    hidden = (silu * pre_up * prob).astype(jnp.bfloat16)
    back_gate = (back_hidden * pre_up * s * (1.0 + pre_gate * (1.0 - s))).astype(jnp.bfloat16)
    back_up = (back_hidden * silu).astype(jnp.bfloat16)
    act_ref[:, :ff] = back_gate
    act_ref[:, ff : 2 * ff] = back_up
    act_ref[:, 2 * ff :] = hidden
    out_ref[:, :cols] = dot(hidden, down_ref[...], NN).astype(out_ref.dtype)
    out_ref[:, cols:] = (
        dot(back_gate, gate_ref[...], NN) + dot(back_up, up_ref[...], NN)
    ).astype(out_ref.dtype)


def call(kernel, out, *args, flops=0, **kw):
    nbytes = sum(a.size * a.dtype.itemsize for a in args)
    return pl.pallas_call(
        kernel,
        out_shape=out,
        in_specs=[VMEM] * len(args),
        out_specs=jax.tree.map(lambda _: VMEM, out),
        compiler_params=pltpu.CompilerParams(vmem_limit_bytes=32 * 2**20),
        cost_estimate=pl.CostEstimate(flops=flops, bytes_accessed=nbytes, transcendentals=0),
        **kw,
    )(*args)


def swap(a, bits):
    n = lax.axis_size("expert")
    return lax.ppermute(a, "expert", [(i, i ^ bits) for i in range(n)])


def dense(tokens, cotangent, expert_ids, gate_probs, w_gate, w_up, w_down, groups):
    tok, cols = tokens.shape
    experts = lax.axis_size("expert")
    ff = w_gate.shape[1]
    gate, up, down = w_gate[0], w_up[0], w_down[0]
    tail = -(-3 * experts // 128) * 128
    onehot = expert_ids[:, :, None] == jnp.arange(experts, dtype=jnp.int32)[None, None, :]
    table = jnp.sum(jnp.where(onehot, gate_probs[:, :, None], 0.0), axis=1)
    hi = table.astype(jnp.bfloat16)
    rest = table - hi.astype(jnp.float32)
    mid = rest.astype(jnp.bfloat16)
    low = (rest - mid.astype(jnp.float32)).astype(jnp.bfloat16)
    fill = jnp.zeros((tok, tail - 3 * experts), jnp.bfloat16)
    packed = jnp.concatenate([tokens, cotangent, hi, mid, low, fill], axis=1)
    lane = lax.broadcasted_iota(jnp.int32, (1, tail), 1)
    pick = ((lane % experts == lax.axis_index("expert")) & (lane < 3 * experts)).astype(jnp.float32)

    pieces = {0: packed}
    for g in groups:
        for k in g:
            if k:
                pieces[k] = swap(packed, 4 * k)
    rows = []
    for g in groups:
        here = jnp.concatenate([pieces[k] for k in g], axis=0) if len(g) > 1 else pieces[g[0]]
        both = jnp.concatenate([here, swap(here, 2)], axis=0)
        rows.append(jnp.concatenate([both, swap(both, 1)], axis=0))
    parts = []
    for r in rows:
        n = r.shape[0]
        parts.append(
            call(
                partial_kernel,
                jax.ShapeDtypeStruct((n, 3 * ff), jnp.bfloat16),
                r, gate, up, down,
                flops=6 * n * ff * cols,
            )
        )
    others = [lax.ppermute(p, "dp", [(0, 1), (1, 0)]) for p in parts]
    outs, acts = [], []
    for r, p, o in zip(rows, parts, others):
        n = r.shape[0]
        out, act = call(
            functools.partial(post_kernel, experts),
            (
                jax.ShapeDtypeStruct((n, 2 * cols), jnp.bfloat16),
                jax.ShapeDtypeStruct((n, 3 * ff), jnp.bfloat16),
            ),
            p, o, r, pick, gate, up, down,
            flops=6 * n * ff * cols,
        )
        outs.append(out)
        acts.append(act)
    total = None
    for g, out in zip(groups, outs):
        n = out.shape[0]
        half = out[: n // 2].astype(jnp.float32) + swap(out[n // 2 :], 1).astype(jnp.float32)
        half = half.astype(jnp.bfloat16)
        quarter = half[: n // 4].astype(jnp.float32) + swap(half[n // 4 :], 2).astype(jnp.float32)
        for j, k in enumerate(g):
            mine = quarter[j * tok : (j + 1) * tok]
            if k:
                mine = swap(mine.astype(jnp.bfloat16), 4 * k).astype(jnp.float32)
            total = mine if total is None else total + mine
    total = total.astype(jnp.bfloat16)
    x_all = jnp.concatenate([r[:, :cols] for r in rows], axis=0)
    d_all = jnp.concatenate([r[:, cols : 2 * cols] for r in rows], axis=0)
    a_all = jnp.concatenate(acts, axis=0)
    gg = dot(a_all[:, :ff], x_all, TN).astype(jnp.bfloat16)
    gu = dot(a_all[:, ff : 2 * ff], x_all, TN).astype(jnp.bfloat16)
    gd = dot(a_all[:, 2 * ff :], d_all, TN).astype(jnp.bfloat16)
    return total[:, :cols], total[:, cols:], gg[None], gu[None], gd[None]


def activate(pre_gate, pre_up, back_hidden):
    sigmas = jax.nn.sigmoid(pre_gate)
    silu_vals = pre_gate * sigmas
    hidden = (silu_vals * pre_up).astype(jnp.bfloat16)
    back_gate = (back_hidden * pre_up * sigmas * (1.0 + pre_gate * (1.0 - sigmas))).astype(
        jnp.bfloat16
    )
    back_up = (back_hidden * silu_vals).astype(jnp.bfloat16)
    return (hidden, back_gate, back_up)


def deliver(outbound):
    return lax.all_to_all(outbound, "expert", split_axis=0, concat_axis=0, tiled=True)


def slotted(tokens, cotangent, expert_ids, gate_probs, w_gate, w_up, w_down):
    tok_rows, columns = tokens.shape
    top_count = expert_ids.shape[1]
    experts = lax.axis_size("expert")
    capacity = min(tok_rows, max(2, 2 * tok_rows * top_count // experts))
    slot_count = experts * capacity
    flat_ids = expert_ids.reshape(-1)
    onehot = (flat_ids[:, None] == jnp.arange(experts, dtype=jnp.int32)[None, :]).astype(jnp.int32)
    before = jnp.cumsum(onehot, axis=0) - onehot
    ranks = jnp.sum(before * onehot, axis=1)
    slot_ids = flat_ids * capacity + ranks
    chosen = (slot_ids[:, None] == jnp.arange(slot_count, dtype=jnp.int32)[None, :]).astype(
        jnp.float32
    )
    chosen = chosen.reshape(tok_rows, top_count, slot_count)
    select = jnp.sum(chosen, axis=1)
    weighted = jnp.sum(chosen * gate_probs[:, :, None], axis=1)
    contract_rows = (((0,), (0,)), ((), ()))
    contract_cols = (((1,), (1,)), ((), ()))
    x_rows = lax.dot_general(
        select.astype(jnp.bfloat16), tokens, contract_rows, preferred_element_type=jnp.float32
    ).astype(jnp.bfloat16)
    back_row = lax.dot_general(
        weighted,
        cotangent.astype(jnp.float32),
        contract_rows,
        precision=lax.Precision.HIGHEST,
        preferred_element_type=jnp.float32,
    ).astype(jnp.bfloat16)
    outbound = jnp.stack([x_rows, back_row], axis=1).reshape(experts, capacity, 2, columns)
    inbound = deliver(outbound).reshape(slot_count, 2, columns)
    x_in = inbound[:, 0]
    d_in = inbound[:, 1]
    gate_mat = w_gate[0]
    up_mat = w_up[0]
    down_mat = w_down[0]
    part_gate = lax.dot_general(x_in, gate_mat, contract_cols, preferred_element_type=jnp.float32)
    part_up = lax.dot_general(x_in, up_mat, contract_cols, preferred_element_type=jnp.float32)
    part_back = lax.dot_general(d_in, down_mat, contract_cols, preferred_element_type=jnp.float32)
    pre_gate, pre_up, back_hidden = (
        lax.psum(part_gate.astype(jnp.bfloat16), "dp").astype(jnp.float32),
        lax.psum(part_up.astype(jnp.bfloat16), "dp").astype(jnp.float32),
        lax.psum(part_back.astype(jnp.bfloat16), "dp").astype(jnp.float32),
    )
    hidden, back_gate, back_up = activate(pre_gate, pre_up, back_hidden)
    expert_out = jnp.dot(hidden, down_mat, preferred_element_type=jnp.float32).astype(jnp.bfloat16)
    back_rows = (
        jnp.dot(back_gate, gate_mat, preferred_element_type=jnp.float32)
        + jnp.dot(back_up, up_mat, preferred_element_type=jnp.float32)
    ).astype(jnp.bfloat16)
    grad_gate = lax.dot_general(
        back_gate, x_in, contract_rows, preferred_element_type=jnp.float32
    ).astype(jnp.bfloat16)
    grad_up = lax.dot_general(
        back_up, x_in, contract_rows, preferred_element_type=jnp.float32
    ).astype(jnp.bfloat16)
    grad_down = lax.dot_general(
        hidden, d_in, contract_rows, preferred_element_type=jnp.float32
    ).astype(jnp.bfloat16)
    homeward = jnp.stack([expert_out, back_rows], axis=1).reshape(experts, capacity, 2, columns)
    returned = deliver(homeward).reshape(slot_count, 2, columns)
    mixed = jnp.dot(
        weighted,
        returned[:, 0].astype(jnp.float32),
        precision=lax.Precision.HIGHEST,
        preferred_element_type=jnp.float32,
    ).astype(jnp.bfloat16)
    grad_tokens = jnp.dot(
        select.astype(jnp.bfloat16), returned[:, 1], preferred_element_type=jnp.float32
    ).astype(jnp.bfloat16)
    return (mixed, grad_tokens, grad_gate[None], grad_up[None], grad_down[None])


def on_device(tokens, cotangent, expert_ids, gate_probs, w_gate, w_up, w_down):
    tok_rows = tokens.shape[0]
    top_count = expert_ids.shape[1]
    experts = lax.axis_size("expert")
    args = (tokens, cotangent, expert_ids, gate_probs, w_gate, w_up, w_down)
    if 2 * tok_rows * top_count >= experts * tok_rows and experts == 16 and lax.axis_size("dp") == 2:
        return dense(*args, groups=((0,), (1,), (2, 3)))
    return slotted(*args)


def solution(mesh):
    in_specs = (
        P("expert", "dp"),
        P("expert", "dp"),
        P("expert", None),
        P("expert", None),
        P("expert", None, "dp"),
        P("expert", None, "dp"),
        P("expert", None, "dp"),
    )
    out_specs = (
        P("expert", "dp"),
        P("expert", "dp"),
        P("expert", None, "dp"),
        P("expert", None, "dp"),
        P("expert", None, "dp"),
    )
    return jax.shard_map(
        on_device, mesh=mesh, in_specs=in_specs, out_specs=out_specs, check_vma=False
    )
```

```python
import functools

import jax
import jax.numpy as jnp
from jax import lax
from jax.experimental import pallas as pl
from jax.experimental.pallas import tpu as pltpu
from jax.sharding import PartitionSpec as P

VMEM = pl.BlockSpec(memory_space=pltpu.VMEM)
HBM = pl.BlockSpec(memory_space=pl.ANY)
NT = (((1,), (1,)), ((), ()))
NN = (((1,), (0,)), ((), ()))
TN = (((0,), (0,)), ((), ()))


def dot(a, b, dims):
    return lax.dot_general(a, b, dims, preferred_element_type=jnp.float32)


def pack_kernel(experts, x_hbm, d_hbm, ids_hbm, probs_hbm, lane_ref, out_ref, pick_ref, ids_ref, probs_ref, sems):
    cols = x_hbm.shape[1]
    top, tok = ids_ref.shape
    tail = out_ref.shape[1] - 2 * cols
    copies = [
        pltpu.make_async_copy(src, dst, sems.at[i])
        for i, (src, dst) in enumerate(
            (
                (ids_hbm, ids_ref),
                (probs_hbm, probs_ref),
                (x_hbm, out_ref.at[:, :cols]),
                (d_hbm, out_ref.at[:, cols : 2 * cols]),
            )
        )
    ]
    for copy in copies:
        copy.start()
    copies[0].wait()
    copies[1].wait()
    number = lax.broadcasted_iota(jnp.int32, (experts, tok), 0)
    table = jnp.zeros((experts, tok), jnp.float32)
    for k in range(top):
        table += jnp.where(ids_ref[k : k + 1, :] == number, probs_ref[k : k + 1, :], 0.0)
    hi = table.astype(jnp.bfloat16).astype(jnp.float32)
    mid = (table - hi).astype(jnp.bfloat16).astype(jnp.float32)
    low = table - hi - mid
    stacked = jnp.concatenate([hi, mid, low], axis=0).astype(jnp.bfloat16)
    spread = (
        lax.broadcasted_iota(jnp.int32, (3 * experts, tail), 0)
        == lax.broadcasted_iota(jnp.int32, (3 * experts, tail), 1)
    ).astype(jnp.bfloat16)
    out_ref[:, 2 * cols :] = dot(stacked, spread, TN).astype(jnp.bfloat16)
    pick_ref[...] = lane_ref[...]
    copies[2].wait()
    copies[3].wait()


def partial_kernel(count, *refs):
    rows, weight_refs, outs = refs[:count], refs[count : count + 3], refs[count + 3 :]
    ff, cols = weight_refs[0].shape
    for i, w_ref in enumerate(weight_refs):
        lo = cols if i == 2 else 0
        side = jnp.concatenate([r[:, lo : lo + cols] for r in rows], axis=0)
        share = dot(side, w_ref[...], NT).astype(jnp.bfloat16)
        start = 0
        for out_ref in outs:
            size = out_ref.shape[0]
            out_ref[:, i * ff : (i + 1) * ff] = share[start : start + size]
            start += size


def post_kernel(own_ref, other_ref, here_ref, there_ref, pick_ref, gate_ref, up_ref, down_ref, out_ref, act_ref):
    ff, cols = gate_ref.shape
    table = jnp.concatenate([here_ref[:, 2 * cols :], there_ref[:, 2 * cols :]], axis=0)
    prob = jnp.sum(table.astype(jnp.float32) * pick_ref[...], axis=1, keepdims=True)
    both = own_ref[...].astype(jnp.float32) + other_ref[...].astype(jnp.float32)
    pre_gate = both[:, :ff]
    pre_up = both[:, ff : 2 * ff]
    back_hidden = both[:, 2 * ff :] * prob
    s = 1.0 / (1.0 + jnp.exp(-pre_gate))
    silu = pre_gate * s
    hidden = (silu * pre_up * prob).astype(jnp.bfloat16)
    back_gate = (back_hidden * pre_up * s * (1.0 + pre_gate * (1.0 - s))).astype(jnp.bfloat16)
    back_up = (back_hidden * silu).astype(jnp.bfloat16)
    act_ref[:, :ff] = back_gate
    act_ref[:, ff : 2 * ff] = back_up
    act_ref[:, 2 * ff :] = hidden
    out_ref[:, :cols] = dot(hidden, down_ref[...], NN).astype(out_ref.dtype)
    out_ref[:, cols:] = (
        dot(back_gate, gate_ref[...], NN) + dot(back_up, up_ref[...], NN)
    ).astype(out_ref.dtype)


def grad_kernel(steps, count, *refs):
    act_refs, row_refs = refs[:count], refs[count:-5]
    outs, block_ref, sems = refs[-5:-2], refs[-2], refs[-1]
    ff, cols = outs[0].shape[1:]
    size = ff // steps
    copies = []
    for i, out_hbm in enumerate(outs):
        lo = cols if i == 2 else 0
        side = jnp.concatenate([r[:, lo : lo + cols] for r in row_refs], axis=0)
        for j in range(steps):
            at = i * ff + j * size
            act = jnp.concatenate([r[:, at : at + size] for r in act_refs], axis=0)
            block_ref[at : at + size, :] = dot(act, side, TN).astype(jnp.bfloat16)
            copy = pltpu.make_async_copy(
                block_ref.at[at : at + size, :],
                out_hbm.at[0, j * size : (j + 1) * size, :],
                sems.at[i * steps + j],
            )
            copy.start()
            copies.append(copy)
    for copy in copies:
        copy.wait()


def hbm(a):
    return pltpu.with_memory_space_constraint(a, pltpu.HBM)


def near(a):
    return pltpu.with_memory_space_constraint(a, pltpu.VMEM)


def call(kernel, out, *args, flops=0, free=(), far=(), mib=16, **kw):
    nbytes = sum(a.size * a.dtype.itemsize for a in args)
    args = [hbm(a) if i in far else a if i in free else near(a) for i, a in enumerate(args)]
    return pl.pallas_call(
        kernel,
        out_shape=jax.tree.map(lambda o: pltpu.VMEM(o.shape, o.dtype), out),
        in_specs=[HBM if i in far else VMEM for i in range(len(args))],
        out_specs=jax.tree.map(lambda _: VMEM, out),
        compiler_params=pltpu.CompilerParams(vmem_limit_bytes=mib * 2**20),
        cost_estimate=pl.CostEstimate(flops=flops, bytes_accessed=nbytes, transcendentals=0),
        **kw,
    )(*args)


def grads(acts, rows, ff, cols):
    steps = ff // 256 if ff % 256 == 0 else 1
    count = len(acts)
    n = sum(a.shape[0] for a in acts)
    shape = jax.ShapeDtypeStruct((1, ff, cols), jnp.bfloat16)
    return pl.pallas_call(
        functools.partial(grad_kernel, steps, count),
        out_shape=(shape,) * 3,
        in_specs=[VMEM] * (count + len(rows)),
        out_specs=(HBM,) * 3,
        scratch_shapes=[
            pltpu.VMEM((3 * ff, cols), jnp.bfloat16),
            pltpu.SemaphoreType.DMA((3 * steps,)),
        ],
        compiler_params=pltpu.CompilerParams(vmem_limit_bytes=24 * 2**20),
        cost_estimate=pl.CostEstimate(
            flops=6 * n * ff * cols, bytes_accessed=6 * ff * cols, transcendentals=0
        ),
    )(*map(near, acts), *map(near, rows))


def swap(a, bits):
    n = lax.axis_size("expert")
    return lax.ppermute(a, "expert", [(i, i ^ bits) for i in range(n)])


def dense(tokens, cotangent, expert_ids, gate_probs, w_gate, w_up, w_down):
    tok, cols = tokens.shape
    experts = lax.axis_size("expert")
    top = expert_ids.shape[1]
    ff = w_gate.shape[1]
    tail = -(-3 * experts // 128) * 128
    bf16 = jnp.bfloat16
    f32 = jnp.float32
    lane = lax.broadcasted_iota(jnp.int32, (1, tail), 1)
    pick = ((lane % experts == lax.axis_index("expert")) & (lane < 3 * experts)).astype(f32)
    own, pick = call(
        functools.partial(pack_kernel, experts),
        (jax.ShapeDtypeStruct((tok, 2 * cols + tail), bf16), jax.ShapeDtypeStruct((1, tail), f32)),
        tokens, cotangent, expert_ids.T, gate_probs.T, pick,
        far=(0, 1, 2, 3),
        free=(4,),
        flops=3 * 10**10,
        scratch_shapes=[
            pltpu.VMEM((top, tok), jnp.int32),
            pltpu.VMEM((top, tok), f32),
            pltpu.SemaphoreType.DMA((4,)),
        ],
    )
    weights = (w_gate[0], w_up[0], w_down[0])

    def shares_of(rows, sizes):
        return call(
            functools.partial(partial_kernel, len(rows)),
            tuple(jax.ShapeDtypeStruct((n, 3 * ff), bf16) for n in sizes),
            *rows, *weights,
            free=tuple(range(len(rows), len(rows) + 3)),
            flops=6 * sum(sizes) * ff * cols,
        )

    def other(share):
        return lax.ppermute(share, "dp", [(0, 1), (1, 0)])

    def post(share, arrived, here, there):
        n = share.shape[0]
        return call(
            post_kernel,
            (jax.ShapeDtypeStruct((n, 2 * cols), bf16), jax.ShapeDtypeStruct((n, 3 * ff), bf16)),
            share, arrived, here, there, pick, *weights,
            free=(4, 5, 6, 7),
            flops=6 * n * ff * cols,
        )

    def fold(a, bits):
        n = a.shape[0] // 2
        return a[:n].astype(f32) + swap(a[n:].astype(bf16), bits).astype(f32)

    def after(a, *b):
        return lax.optimization_barrier((a,) + b)[0]

    n = 4 * tok
    far = range(2, experts // 4)
    own_core = swap(own, 1)
    alone = [swap(own, 4 * k) for k in far]
    here1 = jnp.concatenate([swap(own, 4), swap(own, 6)], axis=0)
    there1 = swap(here1, 1)
    (share1,) = shares_of((here1, there1), (n,))
    other1 = other(share1)
    beside = swap(jnp.concatenate(alone, axis=0), 2)
    *alone, beside, _ = lax.optimization_barrier((*alone, beside, share1))
    here = [
        jnp.concatenate([a, beside[i * tok : (i + 1) * tok]], axis=0) for i, a in enumerate(alone)
    ]
    there = swap(jnp.concatenate(here, axis=0), 1)
    there = [there[2 * i * tok : 2 * (i + 1) * tok] for i in range(len(here))]
    shares = shares_of([r for pair in zip(here, there) for r in pair], (n,) * len(here))
    others = [other(s) for s in shares]
    own_beside = swap(after(own, *shares), 2)
    here0 = jnp.concatenate([own, own_beside], axis=0)
    there0 = jnp.concatenate([own_core, swap(own_beside, 1)], axis=0)
    (share0,) = shares_of((here0, there0), (n,))
    other0 = other(share0)

    out1, act1 = post(share1, after(other1, *shares), here1, there1)
    near = swap(fold(out1, 1).astype(bf16), 4).astype(f32)
    acts, halves, quarters, back = [], [], [], []
    for k, share, arrived, h, t in zip(far, shares, others, here, there):
        out, act = post(share, after(arrived, *halves[-1:]), h, t)
        halves.append(fold(out, 1).astype(bf16))
        quarters.append(fold(halves[-1], 2).astype(bf16))
        back.append(swap(quarters[-1], 4 * k))
        acts.append(act)
    out0, act0 = post(share0, after(other0, quarters[0], halves[-1]), here0, there0)
    total = fold(near + fold(out0, 1), 2)
    for b in back:
        total += b.astype(f32)
    total = total.astype(bf16)
    gg, gu, gd = grads(
        (act0, act1, *acts),
        (here0, there0, here1, there1, *[r for pair in zip(here, there) for r in pair]),
        ff, cols,
    )
    return total[:, :cols], total[:, cols:], gg, gu, gd


def activate(pre_gate, pre_up, back_hidden):
    sigmas = jax.nn.sigmoid(pre_gate)
    silu_vals = pre_gate * sigmas
    hidden = (silu_vals * pre_up).astype(jnp.bfloat16)
    back_gate = (back_hidden * pre_up * sigmas * (1.0 + pre_gate * (1.0 - sigmas))).astype(
        jnp.bfloat16
    )
    back_up = (back_hidden * silu_vals).astype(jnp.bfloat16)
    return (hidden, back_gate, back_up)


def deliver(outbound):
    return lax.all_to_all(outbound, "expert", split_axis=0, concat_axis=0, tiled=True)


def slotted(tokens, cotangent, expert_ids, gate_probs, w_gate, w_up, w_down):
    tok_rows, columns = tokens.shape
    top_count = expert_ids.shape[1]
    experts = lax.axis_size("expert")
    capacity = min(tok_rows, max(2, 2 * tok_rows * top_count // experts))
    slot_count = experts * capacity
    flat_ids = expert_ids.reshape(-1)
    onehot = (flat_ids[:, None] == jnp.arange(experts, dtype=jnp.int32)[None, :]).astype(jnp.int32)
    before = jnp.cumsum(onehot, axis=0) - onehot
    ranks = jnp.sum(before * onehot, axis=1)
    slot_ids = flat_ids * capacity + ranks
    chosen = (slot_ids[:, None] == jnp.arange(slot_count, dtype=jnp.int32)[None, :]).astype(
        jnp.float32
    )
    chosen = chosen.reshape(tok_rows, top_count, slot_count)
    select = jnp.sum(chosen, axis=1)
    weighted = jnp.sum(chosen * gate_probs[:, :, None], axis=1)
    contract_rows = (((0,), (0,)), ((), ()))
    contract_cols = (((1,), (1,)), ((), ()))
    x_rows = lax.dot_general(
        select.astype(jnp.bfloat16), tokens, contract_rows, preferred_element_type=jnp.float32
    ).astype(jnp.bfloat16)
    back_row = lax.dot_general(
        weighted,
        cotangent.astype(jnp.float32),
        contract_rows,
        precision=lax.Precision.HIGHEST,
        preferred_element_type=jnp.float32,
    ).astype(jnp.bfloat16)
    outbound = jnp.stack([x_rows, back_row], axis=1).reshape(experts, capacity, 2, columns)
    inbound = deliver(outbound).reshape(slot_count, 2, columns)
    x_in = inbound[:, 0]
    d_in = inbound[:, 1]
    gate_mat = w_gate[0]
    up_mat = w_up[0]
    down_mat = w_down[0]
    part_gate = lax.dot_general(x_in, gate_mat, contract_cols, preferred_element_type=jnp.float32)
    part_up = lax.dot_general(x_in, up_mat, contract_cols, preferred_element_type=jnp.float32)
    part_back = lax.dot_general(d_in, down_mat, contract_cols, preferred_element_type=jnp.float32)
    pre_gate, pre_up, back_hidden = (
        lax.psum(part_gate.astype(jnp.bfloat16), "dp").astype(jnp.float32),
        lax.psum(part_up.astype(jnp.bfloat16), "dp").astype(jnp.float32),
        lax.psum(part_back.astype(jnp.bfloat16), "dp").astype(jnp.float32),
    )
    hidden, back_gate, back_up = activate(pre_gate, pre_up, back_hidden)
    expert_out = jnp.dot(hidden, down_mat, preferred_element_type=jnp.float32).astype(jnp.bfloat16)
    back_rows = (
        jnp.dot(back_gate, gate_mat, preferred_element_type=jnp.float32)
        + jnp.dot(back_up, up_mat, preferred_element_type=jnp.float32)
    ).astype(jnp.bfloat16)
    grad_gate = lax.dot_general(
        back_gate, x_in, contract_rows, preferred_element_type=jnp.float32
    ).astype(jnp.bfloat16)
    grad_up = lax.dot_general(
        back_up, x_in, contract_rows, preferred_element_type=jnp.float32
    ).astype(jnp.bfloat16)
    grad_down = lax.dot_general(
        hidden, d_in, contract_rows, preferred_element_type=jnp.float32
    ).astype(jnp.bfloat16)
    homeward = jnp.stack([expert_out, back_rows], axis=1).reshape(experts, capacity, 2, columns)
    returned = deliver(homeward).reshape(slot_count, 2, columns)
    mixed = jnp.dot(
        weighted,
        returned[:, 0].astype(jnp.float32),
        precision=lax.Precision.HIGHEST,
        preferred_element_type=jnp.float32,
    ).astype(jnp.bfloat16)
    grad_tokens = jnp.dot(
        select.astype(jnp.bfloat16), returned[:, 1], preferred_element_type=jnp.float32
    ).astype(jnp.bfloat16)
    return (mixed, grad_tokens, grad_gate[None], grad_up[None], grad_down[None])


def on_device(tokens, cotangent, expert_ids, gate_probs, w_gate, w_up, w_down):
    tok_rows = tokens.shape[0]
    top_count = expert_ids.shape[1]
    experts = lax.axis_size("expert")
    args = (tokens, cotangent, expert_ids, gate_probs, w_gate, w_up, w_down)
    pairs = experts // 4
    powers = pairs > 2 and experts & (experts - 1) == 0
    if 2 * tok_rows * top_count >= experts * tok_rows and powers and lax.axis_size("dp") == 2:
        return dense(*args)
    return slotted(*args)


def solution(mesh):
    in_specs = (
        P("expert", "dp"),
        P("expert", "dp"),
        P("expert", None),
        P("expert", None),
        P("expert", None, "dp"),
        P("expert", None, "dp"),
        P("expert", None, "dp"),
    )
    out_specs = (
        P("expert", "dp"),
        P("expert", "dp"),
        P("expert", None, "dp"),
        P("expert", None, "dp"),
        P("expert", None, "dp"),
    )
    return jax.shard_map(
        on_device, mesh=mesh, in_specs=in_specs, out_specs=out_specs, check_vma=False
    )
```

```python
import functools

import jax
import jax.numpy as jnp
from jax import lax
from jax.experimental import pallas as pl
from jax.experimental.pallas import tpu as pltpu
from jax.sharding import PartitionSpec as P

VMEM = pl.BlockSpec(memory_space=pltpu.VMEM)
HBM = pl.BlockSpec(memory_space=pl.ANY)
NT = (((1,), (1,)), ((), ()))
NN = (((1,), (0,)), ((), ()))
TN = (((0,), (0,)), ((), ()))


def dot(a, b, dims):
    return lax.dot_general(a, b, dims, preferred_element_type=jnp.float32)


def pack_kernel(experts, x_hbm, d_hbm, ids_hbm, probs_hbm, lane_ref, out_ref, pick_ref, ids_ref, probs_ref, sems):
    cols = x_hbm.shape[1]
    top, tok = ids_ref.shape
    tail = out_ref.shape[1] - 2 * cols
    copies = [
        pltpu.make_async_copy(src, dst, sems.at[i])
        for i, (src, dst) in enumerate(
            (
                (ids_hbm, ids_ref),
                (probs_hbm, probs_ref),
                (x_hbm, out_ref.at[:, :cols]),
                (d_hbm, out_ref.at[:, cols : 2 * cols]),
            )
        )
    ]
    for copy in copies:
        copy.start()
    copies[0].wait()
    copies[1].wait()
    number = lax.broadcasted_iota(jnp.int32, (experts, tok), 0)
    table = jnp.zeros((experts, tok), jnp.float32)
    for k in range(top):
        table += jnp.where(ids_ref[k : k + 1, :] == number, probs_ref[k : k + 1, :], 0.0)
    hi = table.astype(jnp.bfloat16).astype(jnp.float32)
    mid = (table - hi).astype(jnp.bfloat16).astype(jnp.float32)
    low = table - hi - mid
    stacked = jnp.concatenate([hi, mid, low], axis=0).astype(jnp.bfloat16)
    spread = (
        lax.broadcasted_iota(jnp.int32, (3 * experts, tail), 0)
        == lax.broadcasted_iota(jnp.int32, (3 * experts, tail), 1)
    ).astype(jnp.bfloat16)
    out_ref[:, 2 * cols :] = dot(stacked, spread, TN).astype(jnp.bfloat16)
    pick_ref[...] = lane_ref[...]
    copies[2].wait()
    copies[3].wait()


def partial_kernel(count, *refs):
    rows, weight_refs, outs = refs[:count], refs[count : count + 3], refs[count + 3 :]
    ff, cols = weight_refs[0].shape
    for i, w_ref in enumerate(weight_refs):
        lo = cols if i == 2 else 0
        side = jnp.concatenate([r[:, lo : lo + cols] for r in rows], axis=0)
        share = dot(side, w_ref[...], NT).astype(jnp.bfloat16)
        start = 0
        for out_ref in outs:
            size = out_ref.shape[0]
            out_ref[:, i * ff : (i + 1) * ff] = share[start : start + size]
            start += size


def post_kernel(own_ref, other_ref, here_ref, there_ref, pick_ref, gate_ref, up_ref, down_ref, out_ref, act_ref):
    ff, cols = gate_ref.shape
    table = jnp.concatenate([here_ref[:, 2 * cols :], there_ref[:, 2 * cols :]], axis=0)
    prob = jnp.sum(table.astype(jnp.float32) * pick_ref[...], axis=1, keepdims=True)
    both = own_ref[...].astype(jnp.float32) + other_ref[...].astype(jnp.float32)
    pre_gate = both[:, :ff]
    pre_up = both[:, ff : 2 * ff]
    back_hidden = both[:, 2 * ff :] * prob
    s = 1.0 / (1.0 + jnp.exp(-pre_gate))
    silu = pre_gate * s
    hidden = (silu * pre_up * prob).astype(jnp.bfloat16)
    back_gate = (back_hidden * pre_up * s * (1.0 + pre_gate * (1.0 - s))).astype(jnp.bfloat16)
    back_up = (back_hidden * silu).astype(jnp.bfloat16)
    act_ref[:, :ff] = back_gate
    act_ref[:, ff : 2 * ff] = back_up
    act_ref[:, 2 * ff :] = hidden
    out_ref[:, :cols] = dot(hidden, down_ref[...], NN).astype(out_ref.dtype)
    out_ref[:, cols:] = (
        dot(back_gate, gate_ref[...], NN) + dot(back_up, up_ref[...], NN)
    ).astype(out_ref.dtype)


def grad_kernel(steps, count, *refs):
    act_refs, row_refs = refs[:count], refs[count:-5]
    outs, block_ref, sems = refs[-5:-2], refs[-2], refs[-1]
    ff, cols = outs[0].shape[1:]
    size = ff // steps
    copies = []
    for i, out_hbm in enumerate(outs):
        lo = cols if i == 2 else 0
        side = jnp.concatenate([r[:, lo : lo + cols] for r in row_refs], axis=0)
        for j in range(steps):
            at = i * ff + j * size
            act = jnp.concatenate([r[:, at : at + size] for r in act_refs], axis=0)
            block_ref[at : at + size, :] = dot(act, side, TN).astype(jnp.bfloat16)
            copy = pltpu.make_async_copy(
                block_ref.at[at : at + size, :],
                out_hbm.at[0, j * size : (j + 1) * size, :],
                sems.at[i * steps + j],
            )
            copy.start()
            copies.append(copy)
    for copy in copies:
        copy.wait()


def hbm(a):
    return pltpu.with_memory_space_constraint(a, pltpu.HBM)


def near(a):
    return pltpu.with_memory_space_constraint(a, pltpu.VMEM)


def call(kernel, out, *args, flops=0, free=(), far=(), mib=16, **kw):
    nbytes = sum(a.size * a.dtype.itemsize for a in args)
    args = [hbm(a) if i in far else a if i in free else near(a) for i, a in enumerate(args)]
    return pl.pallas_call(
        kernel,
        out_shape=jax.tree.map(lambda o: pltpu.VMEM(o.shape, o.dtype), out),
        in_specs=[HBM if i in far else VMEM for i in range(len(args))],
        out_specs=jax.tree.map(lambda _: VMEM, out),
        compiler_params=pltpu.CompilerParams(vmem_limit_bytes=mib * 2**20),
        cost_estimate=pl.CostEstimate(flops=flops, bytes_accessed=nbytes, transcendentals=0),
        **kw,
    )(*args)


def grads(acts, rows, ff, cols):
    steps = ff // 256 if ff % 256 == 0 else 1
    count = len(acts)
    n = sum(a.shape[0] for a in acts)
    shape = jax.ShapeDtypeStruct((1, ff, cols), jnp.bfloat16)
    return pl.pallas_call(
        functools.partial(grad_kernel, steps, count),
        out_shape=(shape,) * 3,
        in_specs=[VMEM] * (count + len(rows)),
        out_specs=(HBM,) * 3,
        scratch_shapes=[
            pltpu.VMEM((3 * ff, cols), jnp.bfloat16),
            pltpu.SemaphoreType.DMA((3 * steps,)),
        ],
        compiler_params=pltpu.CompilerParams(vmem_limit_bytes=24 * 2**20),
        cost_estimate=pl.CostEstimate(
            flops=6 * n * ff * cols, bytes_accessed=6 * ff * cols, transcendentals=0
        ),
    )(*map(near, acts), *map(near, rows))


def swap(a, bits):
    n = lax.axis_size("expert")
    return lax.ppermute(a, "expert", [(i, i ^ bits) for i in range(n)])


def dense(tokens, cotangent, expert_ids, gate_probs, w_gate, w_up, w_down):
    tok, cols = tokens.shape
    experts = lax.axis_size("expert")
    top = expert_ids.shape[1]
    ff = w_gate.shape[1]
    tail = -(-3 * experts // 128) * 128
    bf16 = jnp.bfloat16
    f32 = jnp.float32
    lane = lax.broadcasted_iota(jnp.int32, (1, tail), 1)
    pick = ((lane % experts == lax.axis_index("expert")) & (lane < 3 * experts)).astype(f32)
    own, pick = call(
        functools.partial(pack_kernel, experts),
        (jax.ShapeDtypeStruct((tok, 2 * cols + tail), bf16), jax.ShapeDtypeStruct((1, tail), f32)),
        tokens, cotangent, expert_ids.T, gate_probs.T, pick,
        far=(0, 1, 2, 3),
        free=(4,),
        flops=3 * 10**10,
        scratch_shapes=[
            pltpu.VMEM((top, tok), jnp.int32),
            pltpu.VMEM((top, tok), f32),
            pltpu.SemaphoreType.DMA((4,)),
        ],
    )
    weights = (w_gate[0], w_up[0], w_down[0])

    def shares_of(rows, sizes):
        return call(
            functools.partial(partial_kernel, len(rows)),
            tuple(jax.ShapeDtypeStruct((n, 3 * ff), bf16) for n in sizes),
            *rows, *weights,
            free=tuple(range(len(rows), len(rows) + 3)),
            flops=6 * sum(sizes) * ff * cols,
        )

    def other(share):
        return lax.ppermute(share, "dp", [(0, 1), (1, 0)])

    def post(share, arrived, here, there, *first):
        n = share.shape[0]
        mark = after(pick, *first) if first else pick
        return call(
            post_kernel,
            (jax.ShapeDtypeStruct((n, 2 * cols), bf16), jax.ShapeDtypeStruct((n, 3 * ff), bf16)),
            share, arrived, here, there, mark, *weights,
            free=(4, 5, 6, 7),
            flops=6 * n * ff * cols,
        )

    def fold(a, bits):
        n = a.shape[0] // 2
        return a[:n].astype(f32) + swap(a[n:].astype(bf16), bits).astype(f32)

    def after(a, *b):
        return lax.optimization_barrier((a,) + b)[0]

    n = 4 * tok
    far = range(2, experts // 4)
    own_core = swap(own, 1)
    alone = [swap(own, 4 * k) for k in far]
    here1 = jnp.concatenate([swap(own, 4), swap(own, 6)], axis=0)
    there1 = swap(here1, 1)
    (share1,) = shares_of((here1, there1), (n,))
    other1 = other(share1)
    beside = swap(jnp.concatenate(alone, axis=0), 2)
    *alone, beside, _ = lax.optimization_barrier((*alone, beside, share1))
    here = [
        jnp.concatenate([a, beside[i * tok : (i + 1) * tok]], axis=0) for i, a in enumerate(alone)
    ]
    there = swap(jnp.concatenate(here, axis=0), 1)
    there = [there[2 * i * tok : 2 * (i + 1) * tok] for i in range(len(here))]
    shares = shares_of([r for pair in zip(here, there) for r in pair], (n,) * len(here))
    others = [other(s) for s in shares]
    own_beside = swap(after(own, *shares), 2)
    here0 = jnp.concatenate([own, own_beside], axis=0)
    there0 = jnp.concatenate([own_core, swap(own_beside, 1)], axis=0)
    (share0,) = shares_of((here0, there0), (n,))
    other0 = other(share0)

    out1, act1 = post(share1, other1, here1, there1, *shares)
    near1 = swap(fold(out1, 1).astype(bf16), 4)
    joined = [near1]
    acts, quarters, back = [], [], []
    for i, k in enumerate(far):
        out, act = post(shares[i], others[i], here[i], there[i], *((near1,) if i else ()))
        acts.append(act)
        half = fold(out, 1).astype(bf16)
        if i < len(far) - 1:
            quarters.append(fold(half, 2).astype(bf16))
            back.append(swap(quarters[-1], 4 * k))
        else:
            joined.append(swap(half, 4 * k))
    out0, act0 = post(share0, other0, here0, there0, *quarters)
    total = joined[0].astype(f32) + fold(out0, 1)
    for a in joined[1:]:
        total += a.astype(f32)
    total = fold(total, 2)
    for a in back:
        total += a.astype(f32)
    total = total.astype(bf16)
    gg, gu, gd = grads(
        (act0, act1, *acts),
        (here0, there0, here1, there1, *[r for pair in zip(here, there) for r in pair]),
        ff, cols,
    )
    return total[:, :cols], total[:, cols:], gg, gu, gd


def activate(pre_gate, pre_up, back_hidden):
    sigmas = jax.nn.sigmoid(pre_gate)
    silu_vals = pre_gate * sigmas
    hidden = (silu_vals * pre_up).astype(jnp.bfloat16)
    back_gate = (back_hidden * pre_up * sigmas * (1.0 + pre_gate * (1.0 - sigmas))).astype(
        jnp.bfloat16
    )
    back_up = (back_hidden * silu_vals).astype(jnp.bfloat16)
    return (hidden, back_gate, back_up)


def deliver(outbound):
    return lax.all_to_all(outbound, "expert", split_axis=0, concat_axis=0, tiled=True)


def slotted(tokens, cotangent, expert_ids, gate_probs, w_gate, w_up, w_down):
    tok_rows, columns = tokens.shape
    top_count = expert_ids.shape[1]
    experts = lax.axis_size("expert")
    capacity = min(tok_rows, max(2, 2 * tok_rows * top_count // experts))
    slot_count = experts * capacity
    flat_ids = expert_ids.reshape(-1)
    onehot = (flat_ids[:, None] == jnp.arange(experts, dtype=jnp.int32)[None, :]).astype(jnp.int32)
    before = jnp.cumsum(onehot, axis=0) - onehot
    ranks = jnp.sum(before * onehot, axis=1)
    slot_ids = flat_ids * capacity + ranks
    chosen = (slot_ids[:, None] == jnp.arange(slot_count, dtype=jnp.int32)[None, :]).astype(
        jnp.float32
    )
    chosen = chosen.reshape(tok_rows, top_count, slot_count)
    select = jnp.sum(chosen, axis=1)
    weighted = jnp.sum(chosen * gate_probs[:, :, None], axis=1)
    contract_rows = (((0,), (0,)), ((), ()))
    contract_cols = (((1,), (1,)), ((), ()))
    x_rows = lax.dot_general(
        select.astype(jnp.bfloat16), tokens, contract_rows, preferred_element_type=jnp.float32
    ).astype(jnp.bfloat16)
    back_row = lax.dot_general(
        weighted,
        cotangent.astype(jnp.float32),
        contract_rows,
        precision=lax.Precision.HIGHEST,
        preferred_element_type=jnp.float32,
    ).astype(jnp.bfloat16)
    outbound = jnp.stack([x_rows, back_row], axis=1).reshape(experts, capacity, 2, columns)
    inbound = deliver(outbound).reshape(slot_count, 2, columns)
    x_in = inbound[:, 0]
    d_in = inbound[:, 1]
    gate_mat = w_gate[0]
    up_mat = w_up[0]
    down_mat = w_down[0]
    part_gate = lax.dot_general(x_in, gate_mat, contract_cols, preferred_element_type=jnp.float32)
    part_up = lax.dot_general(x_in, up_mat, contract_cols, preferred_element_type=jnp.float32)
    part_back = lax.dot_general(d_in, down_mat, contract_cols, preferred_element_type=jnp.float32)
    pre_gate, pre_up, back_hidden = (
        lax.psum(part_gate.astype(jnp.bfloat16), "dp").astype(jnp.float32),
        lax.psum(part_up.astype(jnp.bfloat16), "dp").astype(jnp.float32),
        lax.psum(part_back.astype(jnp.bfloat16), "dp").astype(jnp.float32),
    )
    hidden, back_gate, back_up = activate(pre_gate, pre_up, back_hidden)
    expert_out = jnp.dot(hidden, down_mat, preferred_element_type=jnp.float32).astype(jnp.bfloat16)
    back_rows = (
        jnp.dot(back_gate, gate_mat, preferred_element_type=jnp.float32)
        + jnp.dot(back_up, up_mat, preferred_element_type=jnp.float32)
    ).astype(jnp.bfloat16)
    grad_gate = lax.dot_general(
        back_gate, x_in, contract_rows, preferred_element_type=jnp.float32
    ).astype(jnp.bfloat16)
    grad_up = lax.dot_general(
        back_up, x_in, contract_rows, preferred_element_type=jnp.float32
    ).astype(jnp.bfloat16)
    grad_down = lax.dot_general(
        hidden, d_in, contract_rows, preferred_element_type=jnp.float32
    ).astype(jnp.bfloat16)
    homeward = jnp.stack([expert_out, back_rows], axis=1).reshape(experts, capacity, 2, columns)
    returned = deliver(homeward).reshape(slot_count, 2, columns)
    mixed = jnp.dot(
        weighted,
        returned[:, 0].astype(jnp.float32),
        precision=lax.Precision.HIGHEST,
        preferred_element_type=jnp.float32,
    ).astype(jnp.bfloat16)
    grad_tokens = jnp.dot(
        select.astype(jnp.bfloat16), returned[:, 1], preferred_element_type=jnp.float32
    ).astype(jnp.bfloat16)
    return (mixed, grad_tokens, grad_gate[None], grad_up[None], grad_down[None])


def on_device(tokens, cotangent, expert_ids, gate_probs, w_gate, w_up, w_down):
    tok_rows = tokens.shape[0]
    top_count = expert_ids.shape[1]
    experts = lax.axis_size("expert")
    args = (tokens, cotangent, expert_ids, gate_probs, w_gate, w_up, w_down)
    pairs = experts // 4
    powers = pairs > 2 and experts & (experts - 1) == 0
    if 2 * tok_rows * top_count >= experts * tok_rows and powers and lax.axis_size("dp") == 2:
        return dense(*args)
    return slotted(*args)


def solution(mesh):
    in_specs = (
        P("expert", "dp"),
        P("expert", "dp"),
        P("expert", None),
        P("expert", None),
        P("expert", None, "dp"),
        P("expert", None, "dp"),
        P("expert", None, "dp"),
    )
    out_specs = (
        P("expert", "dp"),
        P("expert", "dp"),
        P("expert", None, "dp"),
        P("expert", None, "dp"),
        P("expert", None, "dp"),
    )
    return jax.shard_map(
        on_device, mesh=mesh, in_specs=in_specs, out_specs=out_specs, check_vma=False
    )
```

```python
import functools

import jax
import jax.numpy as jnp
from jax import lax
from jax.experimental import pallas as pl
from jax.experimental.pallas import tpu as pltpu
from jax.sharding import PartitionSpec as P

VMEM = pl.BlockSpec(memory_space=pltpu.VMEM)
HBM = pl.BlockSpec(memory_space=pl.ANY)
NT = (((1,), (1,)), ((), ()))
NN = (((1,), (0,)), ((), ()))
TN = (((0,), (0,)), ((), ()))


def dot(a, b, dims):
    return lax.dot_general(a, b, dims, preferred_element_type=jnp.float32)


def pack_kernel(experts, x_hbm, d_hbm, ids_hbm, probs_hbm, lane_ref, out_ref, pick_ref, ids_ref, probs_ref, sems):
    cols = x_hbm.shape[1]
    top, tok = ids_ref.shape
    tail = out_ref.shape[1] - 2 * cols
    copies = [
        pltpu.make_async_copy(src, dst, sems.at[i])
        for i, (src, dst) in enumerate(
            (
                (ids_hbm, ids_ref),
                (probs_hbm, probs_ref),
                (x_hbm, out_ref.at[:, :cols]),
                (d_hbm, out_ref.at[:, cols : 2 * cols]),
            )
        )
    ]
    for copy in copies:
        copy.start()
    copies[0].wait()
    copies[1].wait()
    number = lax.broadcasted_iota(jnp.int32, (experts, tok), 0)
    table = jnp.zeros((experts, tok), jnp.float32)
    for k in range(top):
        table += jnp.where(ids_ref[k : k + 1, :] == number, probs_ref[k : k + 1, :], 0.0)
    hi = table.astype(jnp.bfloat16).astype(jnp.float32)
    mid = (table - hi).astype(jnp.bfloat16).astype(jnp.float32)
    low = table - hi - mid
    stacked = jnp.concatenate([hi, mid, low], axis=0).astype(jnp.bfloat16)
    spread = (
        lax.broadcasted_iota(jnp.int32, (3 * experts, tail), 0)
        == lax.broadcasted_iota(jnp.int32, (3 * experts, tail), 1)
    ).astype(jnp.bfloat16)
    out_ref[:, 2 * cols :] = dot(stacked, spread, TN).astype(jnp.bfloat16)
    pick_ref[...] = lane_ref[...]
    copies[2].wait()
    copies[3].wait()


def partial_kernel(count, *refs):
    rows, weight_refs, outs = refs[:count], refs[count : count + 3], refs[count + 3 :]
    ff, cols = weight_refs[0].shape
    for i, w_ref in enumerate(weight_refs):
        lo = cols if i == 2 else 0
        side = jnp.concatenate([r[:, lo : lo + cols] for r in rows], axis=0)
        share = dot(side, w_ref[...], NT).astype(jnp.bfloat16)
        start = 0
        for out_ref in outs:
            size = out_ref.shape[0]
            out_ref[:, i * ff : (i + 1) * ff] = share[start : start + size]
            start += size


def post_kernel(own_ref, other_ref, here_ref, there_ref, pick_ref, gate_ref, up_ref, down_ref, out_ref, act_ref):
    ff, cols = gate_ref.shape
    table = jnp.concatenate([here_ref[:, 2 * cols :], there_ref[:, 2 * cols :]], axis=0)
    prob = jnp.sum(table.astype(jnp.float32) * pick_ref[...], axis=1, keepdims=True)
    both = own_ref[...].astype(jnp.float32) + other_ref[...].astype(jnp.float32)
    pre_gate = both[:, :ff]
    pre_up = both[:, ff : 2 * ff]
    back_hidden = both[:, 2 * ff :] * prob
    s = 1.0 / (1.0 + jnp.exp(-pre_gate))
    silu = pre_gate * s
    hidden = (silu * pre_up * prob).astype(jnp.bfloat16)
    back_gate = (back_hidden * pre_up * s * (1.0 + pre_gate * (1.0 - s))).astype(jnp.bfloat16)
    back_up = (back_hidden * silu).astype(jnp.bfloat16)
    act_ref[:, :ff] = back_gate
    act_ref[:, ff : 2 * ff] = back_up
    act_ref[:, 2 * ff :] = hidden
    out_ref[:, :cols] = dot(hidden, down_ref[...], NN).astype(out_ref.dtype)
    out_ref[:, cols:] = (
        dot(back_gate, gate_ref[...], NN) + dot(back_up, up_ref[...], NN)
    ).astype(out_ref.dtype)


def grad_kernel(steps, count, *refs):
    act_refs, row_refs = refs[:count], refs[count:-5]
    outs, block_ref, sems = refs[-5:-2], refs[-2], refs[-1]
    ff, cols = outs[0].shape[1:]
    size = ff // steps
    copies = []
    for i, out_hbm in enumerate(outs):
        lo = cols if i == 2 else 0
        side = jnp.concatenate([r[:, lo : lo + cols] for r in row_refs], axis=0)
        for j in range(steps):
            at = i * ff + j * size
            act = jnp.concatenate([r[:, at : at + size] for r in act_refs], axis=0)
            block_ref[at : at + size, :] = dot(act, side, TN).astype(jnp.bfloat16)
            copy = pltpu.make_async_copy(
                block_ref.at[at : at + size, :],
                out_hbm.at[0, j * size : (j + 1) * size, :],
                sems.at[i * steps + j],
            )
            copy.start()
            copies.append(copy)
    for copy in copies:
        copy.wait()


def hbm(a):
    return pltpu.with_memory_space_constraint(a, pltpu.HBM)


def near(a):
    return pltpu.with_memory_space_constraint(a, pltpu.VMEM)


def call(kernel, out, *args, flops=0, free=(), far=(), mib=16, **kw):
    nbytes = sum(a.size * a.dtype.itemsize for a in args)
    args = [hbm(a) if i in far else a if i in free else near(a) for i, a in enumerate(args)]
    return pl.pallas_call(
        kernel,
        out_shape=jax.tree.map(lambda o: pltpu.VMEM(o.shape, o.dtype), out),
        in_specs=[HBM if i in far else VMEM for i in range(len(args))],
        out_specs=jax.tree.map(lambda _: VMEM, out),
        compiler_params=pltpu.CompilerParams(vmem_limit_bytes=mib * 2**20),
        cost_estimate=pl.CostEstimate(flops=flops, bytes_accessed=nbytes, transcendentals=0),
        **kw,
    )(*args)


def grads(acts, rows, ff, cols):
    steps = ff // 256 if ff % 256 == 0 else 1
    count = len(acts)
    n = sum(a.shape[0] for a in acts)
    shape = jax.ShapeDtypeStruct((1, ff, cols), jnp.bfloat16)
    return pl.pallas_call(
        functools.partial(grad_kernel, steps, count),
        out_shape=(shape,) * 3,
        in_specs=[VMEM] * (count + len(rows)),
        out_specs=(HBM,) * 3,
        scratch_shapes=[
            pltpu.VMEM((3 * ff, cols), jnp.bfloat16),
            pltpu.SemaphoreType.DMA((3 * steps,)),
        ],
        compiler_params=pltpu.CompilerParams(vmem_limit_bytes=24 * 2**20),
        cost_estimate=pl.CostEstimate(
            flops=6 * n * ff * cols, bytes_accessed=6 * ff * cols, transcendentals=0
        ),
    )(*map(near, acts), *map(near, rows))


def swap(a, bits):
    n = lax.axis_size("expert")
    return lax.ppermute(a, "expert", [(i, i ^ bits) for i in range(n)])


def dense(tokens, cotangent, expert_ids, gate_probs, w_gate, w_up, w_down):
    tok, cols = tokens.shape
    experts = lax.axis_size("expert")
    top = expert_ids.shape[1]
    ff = w_gate.shape[1]
    tail = -(-3 * experts // 128) * 128
    bf16 = jnp.bfloat16
    f32 = jnp.float32
    lane = lax.broadcasted_iota(jnp.int32, (1, tail), 1)
    pick = ((lane % experts == lax.axis_index("expert")) & (lane < 3 * experts)).astype(f32)
    own, pick = call(
        functools.partial(pack_kernel, experts),
        (jax.ShapeDtypeStruct((tok, 2 * cols + tail), bf16), jax.ShapeDtypeStruct((1, tail), f32)),
        tokens, cotangent, expert_ids.T, gate_probs.T, pick,
        far=(0, 1, 2, 3),
        free=(4,),
        flops=3 * 10**10,
        scratch_shapes=[
            pltpu.VMEM((top, tok), jnp.int32),
            pltpu.VMEM((top, tok), f32),
            pltpu.SemaphoreType.DMA((4,)),
        ],
    )
    weights = (w_gate[0], w_up[0], w_down[0])

    def shares_of(rows, sizes):
        return call(
            functools.partial(partial_kernel, len(rows)),
            tuple(jax.ShapeDtypeStruct((n, 3 * ff), bf16) for n in sizes),
            *rows, *weights,
            free=tuple(range(len(rows), len(rows) + 3)),
            flops=6 * sum(sizes) * ff * cols,
        )

    def other(share):
        return lax.ppermute(share, "dp", [(0, 1), (1, 0)])

    def post(share, arrived, here, there, *first):
        n = share.shape[0]
        mark = after(pick, *first) if first else pick
        return call(
            post_kernel,
            (jax.ShapeDtypeStruct((n, 2 * cols), bf16), jax.ShapeDtypeStruct((n, 3 * ff), bf16)),
            share, arrived, here, there, mark, *weights,
            free=(4, 5, 6, 7),
            flops=6 * n * ff * cols,
        )

    def fold(a, bits):
        n = a.shape[0] // 2
        return a[:n].astype(f32) + swap(a[n:].astype(bf16), bits).astype(f32)

    def after(a, *b):
        return lax.optimization_barrier((a,) + b)[0]

    n = 4 * tok
    far = range(2, experts // 4)
    own_core = swap(own, 1)
    alone = [swap(own, 4 * k) for k in far]
    here1 = jnp.concatenate([swap(own, 4), swap(own, 6)], axis=0)
    there1 = swap(here1, 1)
    (share1,) = shares_of((here1, there1), (n,))
    other1 = other(share1)
    beside = swap(jnp.concatenate(alone, axis=0), 2)
    *alone, beside, _ = lax.optimization_barrier((*alone, beside, share1))
    here = [
        jnp.concatenate([a, beside[i * tok : (i + 1) * tok]], axis=0) for i, a in enumerate(alone)
    ]
    there = swap(jnp.concatenate(here, axis=0), 1)
    there = [there[2 * i * tok : 2 * (i + 1) * tok] for i in range(len(here))]
    shares = shares_of([r for pair in zip(here, there) for r in pair], (n,) * len(here))
    others = [other(s) for s in shares]
    own_beside = swap(after(own, *shares), 2)
    here0 = jnp.concatenate([own, own_beside], axis=0)
    there0 = jnp.concatenate([own_core, swap(own_beside, 1)], axis=0)
    (share0,) = shares_of((here0, there0), (n,))
    other0 = other(share0)

    out1, act1 = post(share1, other1, here1, there1, *shares)
    near1 = swap(fold(out1, 1).astype(bf16), 4)
    joined = [near1]
    acts, quarters, back = [], [], []
    for i, k in enumerate(far):
        out, act = post(shares[i], others[i], here[i], there[i], *((near1, share0) if i else ()))
        acts.append(act)
        half = fold(out, 1).astype(bf16)
        if i < len(far) - 1:
            quarters.append(fold(half, 2).astype(bf16))
            back.append(swap(quarters[-1], 4 * k))
        else:
            joined.append(swap(half, 4 * k))
    out0, act0 = post(share0, other0, here0, there0, *quarters)
    total = joined[0].astype(f32) + fold(out0, 1)
    for a in joined[1:]:
        total += a.astype(f32)
    total = fold(total, 2)
    for a in back:
        total += a.astype(f32)
    total = total.astype(bf16)
    gg, gu, gd = grads(
        (act0, act1, *acts),
        (here0, there0, here1, there1, *[r for pair in zip(here, there) for r in pair]),
        ff, cols,
    )
    return total[:, :cols], total[:, cols:], gg, gu, gd


def activate(pre_gate, pre_up, back_hidden):
    sigmas = jax.nn.sigmoid(pre_gate)
    silu_vals = pre_gate * sigmas
    hidden = (silu_vals * pre_up).astype(jnp.bfloat16)
    back_gate = (back_hidden * pre_up * sigmas * (1.0 + pre_gate * (1.0 - sigmas))).astype(
        jnp.bfloat16
    )
    back_up = (back_hidden * silu_vals).astype(jnp.bfloat16)
    return (hidden, back_gate, back_up)


def deliver(outbound):
    return lax.all_to_all(outbound, "expert", split_axis=0, concat_axis=0, tiled=True)


def slotted(tokens, cotangent, expert_ids, gate_probs, w_gate, w_up, w_down):
    tok_rows, columns = tokens.shape
    top_count = expert_ids.shape[1]
    experts = lax.axis_size("expert")
    capacity = min(tok_rows, max(2, 2 * tok_rows * top_count // experts))
    slot_count = experts * capacity
    flat_ids = expert_ids.reshape(-1)
    onehot = (flat_ids[:, None] == jnp.arange(experts, dtype=jnp.int32)[None, :]).astype(jnp.int32)
    before = jnp.cumsum(onehot, axis=0) - onehot
    ranks = jnp.sum(before * onehot, axis=1)
    slot_ids = flat_ids * capacity + ranks
    chosen = (slot_ids[:, None] == jnp.arange(slot_count, dtype=jnp.int32)[None, :]).astype(
        jnp.float32
    )
    chosen = chosen.reshape(tok_rows, top_count, slot_count)
    select = jnp.sum(chosen, axis=1)
    weighted = jnp.sum(chosen * gate_probs[:, :, None], axis=1)
    contract_rows = (((0,), (0,)), ((), ()))
    contract_cols = (((1,), (1,)), ((), ()))
    x_rows = lax.dot_general(
        select.astype(jnp.bfloat16), tokens, contract_rows, preferred_element_type=jnp.float32
    ).astype(jnp.bfloat16)
    back_row = lax.dot_general(
        weighted,
        cotangent.astype(jnp.float32),
        contract_rows,
        precision=lax.Precision.HIGHEST,
        preferred_element_type=jnp.float32,
    ).astype(jnp.bfloat16)
    outbound = jnp.stack([x_rows, back_row], axis=1).reshape(experts, capacity, 2, columns)
    inbound = deliver(outbound).reshape(slot_count, 2, columns)
    x_in = inbound[:, 0]
    d_in = inbound[:, 1]
    gate_mat = w_gate[0]
    up_mat = w_up[0]
    down_mat = w_down[0]
    part_gate = lax.dot_general(x_in, gate_mat, contract_cols, preferred_element_type=jnp.float32)
    part_up = lax.dot_general(x_in, up_mat, contract_cols, preferred_element_type=jnp.float32)
    part_back = lax.dot_general(d_in, down_mat, contract_cols, preferred_element_type=jnp.float32)
    pre_gate, pre_up, back_hidden = (
        lax.psum(part_gate.astype(jnp.bfloat16), "dp").astype(jnp.float32),
        lax.psum(part_up.astype(jnp.bfloat16), "dp").astype(jnp.float32),
        lax.psum(part_back.astype(jnp.bfloat16), "dp").astype(jnp.float32),
    )
    hidden, back_gate, back_up = activate(pre_gate, pre_up, back_hidden)
    expert_out = jnp.dot(hidden, down_mat, preferred_element_type=jnp.float32).astype(jnp.bfloat16)
    back_rows = (
        jnp.dot(back_gate, gate_mat, preferred_element_type=jnp.float32)
        + jnp.dot(back_up, up_mat, preferred_element_type=jnp.float32)
    ).astype(jnp.bfloat16)
    grad_gate = lax.dot_general(
        back_gate, x_in, contract_rows, preferred_element_type=jnp.float32
    ).astype(jnp.bfloat16)
    grad_up = lax.dot_general(
        back_up, x_in, contract_rows, preferred_element_type=jnp.float32
    ).astype(jnp.bfloat16)
    grad_down = lax.dot_general(
        hidden, d_in, contract_rows, preferred_element_type=jnp.float32
    ).astype(jnp.bfloat16)
    homeward = jnp.stack([expert_out, back_rows], axis=1).reshape(experts, capacity, 2, columns)
    returned = deliver(homeward).reshape(slot_count, 2, columns)
    mixed = jnp.dot(
        weighted,
        returned[:, 0].astype(jnp.float32),
        precision=lax.Precision.HIGHEST,
        preferred_element_type=jnp.float32,
    ).astype(jnp.bfloat16)
    grad_tokens = jnp.dot(
        select.astype(jnp.bfloat16), returned[:, 1], preferred_element_type=jnp.float32
    ).astype(jnp.bfloat16)
    return (mixed, grad_tokens, grad_gate[None], grad_up[None], grad_down[None])


def on_device(tokens, cotangent, expert_ids, gate_probs, w_gate, w_up, w_down):
    tok_rows = tokens.shape[0]
    top_count = expert_ids.shape[1]
    experts = lax.axis_size("expert")
    args = (tokens, cotangent, expert_ids, gate_probs, w_gate, w_up, w_down)
    pairs = experts // 4
    powers = pairs > 2 and experts & (experts - 1) == 0
    if 2 * tok_rows * top_count >= experts * tok_rows and powers and lax.axis_size("dp") == 2:
        return dense(*args)
    return slotted(*args)


def solution(mesh):
    in_specs = (
        P("expert", "dp"),
        P("expert", "dp"),
        P("expert", None),
        P("expert", None),
        P("expert", None, "dp"),
        P("expert", None, "dp"),
        P("expert", None, "dp"),
    )
    out_specs = (
        P("expert", "dp"),
        P("expert", "dp"),
        P("expert", None, "dp"),
        P("expert", None, "dp"),
        P("expert", None, "dp"),
    )
    return jax.shard_map(
        on_device, mesh=mesh, in_specs=in_specs, out_specs=out_specs, check_vma=False
    )
```
